256 devices in a mesh: gx: 16 (over x, y_lo, core), gy: 16 (over y_hi, z).
Axes of the slice: x: 4, y: 4 (y_hi: 2, y_lo: 2; y = y_hi * 2 + y_lo), z: 8, core: 2. Of those that a mesh axis runs over, the one named last changes fastest.
Arguments:
- tokens: bfloat16 [256, 8192], P('gx', 'gy'), may hold values from -6 to 6
- seeds: int32 [256, 4], P('gx'), may hold values from 0 to 63
- bank: bfloat16 [64, 8192], P(None, 'gy'), may hold values from -6 to 6
- teacher: bfloat16 [256, 4, 8192], P('gx', None, 'gy'), may hold values from -6 to 6
- gate_w: bfloat16 [8192, 14336], P('gy', 'gx'), may hold values from -0.0625 to 0.0625
- up_w: bfloat16 [8192, 14336], P('gy', 'gx'), may hold values from -0.0625 to 0.0625
- down_w: bfloat16 [14336, 8192], P('gx', 'gy'), may hold values from -0.046875 to 0.046875
Outputs:
- student_out: bfloat16 [256, 8192], P('gx', 'gy')
- grad_gate: bfloat16 [8192, 14336], P('gy', 'gx')
- grad_up: bfloat16 [8192, 14336], P('gy', 'gx')
- grad_down: bfloat16 [14336, 8192], P('gx', 'gy')
The draws below stay inside these ranges and needn't reach their ends.
Inputs may be any that keep to these rules, and one draw needn't show every extreme that they name: `seeds`: each seed picks one row of bank.
All inputs are finite; a program needn't handle non-finite values.
Results may differ from the reference program's by a relative error of at most 0.0075.
Values may be sent and summed in bfloat16 or wider, within the bound.
A program may use at most 64 MiB of HBM per device.

```python
import math
import jax
import jax.numpy as jnp

D = 8192
FF = 14336
PROBES = 4
NBANK = 64
TOKENS = 256


def place_ends(drawn, own_key, smallest, largest):
    spot = [jax.random.randint(jax.random.fold_in(own_key, axis), (), 0, length) for axis, length in enumerate(drawn.shape)]
    main_axis = drawn.shape.index(max(drawn.shape))
    beside = spot[:main_axis] + [(spot[main_axis] + 1) % drawn.shape[main_axis]] + spot[main_axis + 1:]
    return drawn.at[tuple(spot)].set(smallest).at[tuple(beside)].set(largest)


def level_of(own_key, shape, shards, low, top_value):
    level = 1.0
    for position, blocks in shards:
        heights = jax.random.uniform(jax.random.fold_in(jax.random.fold_in(own_key, 6), position), (blocks,), jnp.float32, low / len(shards), top_value / len(shards))
        level = level * jnp.repeat(jnp.exp(heights), shape[position] // blocks).reshape((-1,) + (1,) * (len(shape) - 1 - position))
    return level


def centred(key, shape, scale, most, split=(), held_as=jnp.bfloat16):
    level = level_of(key, shape, split, -0.22, 0.18) if split else 1.0
    drawn = jax.random.normal(key, shape, jnp.float32) * scale * level
    return jnp.minimum(jnp.maximum(drawn, -most), most).astype(held_as)


def setup_inputs(seed: int = 0) -> dict:
    keys = jax.random.split(jax.random.key(seed), 8)
    tokens = centred(keys[0], (TOKENS, D), 1.0, 6.0, ((0, 16), (1, 16)))
    seeds = place_ends(jax.random.randint(keys[1], (TOKENS, PROBES), 0, NBANK), jax.random.fold_in(keys[1], 1), 0, NBANK - 1).astype(jnp.int32)
    bank = centred(keys[2], (NBANK, D), 1.0, 6.0, ((1, 16),))
    teacher = centred(keys[3], (TOKENS, PROBES, D), 1.0, 6.0, ((0, 16), (2, 16)))
    gate_w = centred(keys[4], (D, FF), D ** -0.5, 0.0625, ((0, 16), (1, 16)))
    up_w = centred(keys[5], (D, FF), D ** -0.5, 0.0625, ((0, 16), (1, 16)))
    down_w = centred(keys[6], (FF, D), FF ** -0.5, 0.046875, ((0, 16), (1, 16)))
    return {"tokens": tokens, "seeds": seeds, "bank": bank, "teacher": teacher, "gate_w": gate_w, "up_w": up_w, "down_w": down_w}


def hidden_map(pre_gate, pre_up):
    g = pre_gate[:, 0]
    u = pre_up[:, 0]
    s = jax.nn.sigmoid(g)
    act = g * s
    slope = s * (1.0 + g * (1.0 - s))
    first = act * u
    rest = slope[:, None] * pre_gate[:, 1:] * u[:, None] + act[:, None] * pre_up[:, 1:]
    return jnp.concatenate([first[:, None], rest], axis=1)

def reference(tokens, seeds, bank, teacher, gate_w, up_w, down_w):
    onehot = (seeds[..., None] == jnp.arange(NBANK, dtype=jnp.int32)).astype(jnp.bfloat16)
    tangents = jnp.dot(onehot.reshape(-1, NBANK), bank, preferred_element_type=jnp.float32)
    tangents = tangents.astype(jnp.bfloat16).reshape(TOKENS, PROBES, D)
    stacked = jnp.concatenate([tokens[:, None, :], tangents], axis=1)
    flat = stacked.reshape(-1, D)
    pre_gate = jnp.dot(flat, gate_w, preferred_element_type=jnp.float32).reshape(TOKENS, PROBES + 1, FF)
    pre_up = jnp.dot(flat, up_w, preferred_element_type=jnp.float32).reshape(TOKENS, PROBES + 1, FF)
    hidden, pullback = jax.vjp(hidden_map, pre_gate, pre_up)
    hidden = hidden.astype(jnp.bfloat16)
    outputs = jnp.dot(hidden.reshape(-1, FF), down_w, preferred_element_type=jnp.float32).reshape(TOKENS, PROBES + 1, D)
    student_out = outputs[:, 0].astype(jnp.bfloat16)
    out_cot = ((outputs[:, 1:] - teacher.astype(jnp.float32)) / math.sqrt(PROBES * TOKENS)).astype(jnp.bfloat16)
    grad_down = jnp.dot(hidden[:, 1:].reshape(-1, FF).T, out_cot.reshape(-1, D), preferred_element_type=jnp.float32).astype(jnp.bfloat16)
    hid_cot = jnp.dot(out_cot.reshape(-1, D), down_w.T, preferred_element_type=jnp.float32).reshape(TOKENS, PROBES, FF)
    zero_slot = jnp.zeros((TOKENS, 1, FF), dtype=jnp.float32)
    gate_cot, up_cot = pullback(jnp.concatenate([zero_slot, hid_cot], axis=1))
    gate_cot = gate_cot.astype(jnp.bfloat16).reshape(-1, FF)
    up_cot = up_cot.astype(jnp.bfloat16).reshape(-1, FF)
    grad_gate = jnp.dot(flat.T, gate_cot, preferred_element_type=jnp.float32).astype(jnp.bfloat16)
    grad_up = jnp.dot(flat.T, up_cot, preferred_element_type=jnp.float32).astype(jnp.bfloat16)
    return (student_out, grad_gate, grad_up, grad_down)
```

```python
import math

import jax
import jax.numpy as jnp
from jax import lax
from jax.sharding import PartitionSpec as P

F32 = jnp.float32
BF16 = jnp.bfloat16


def dot(a, b):
    return jnp.dot(a, b, preferred_element_type=F32)


def contract_rows(left, right):
    return lax.dot_general(left, right, (((0,), (0,)), ((), ())), preferred_element_type=F32)


def on_device(tokens, seeds, bank, teacher, gate_w, up_w, down_w):
    nbank = bank.shape[0]
    probes = seeds.shape[1]
    ff = gate_w.shape[1]
    width = tokens.shape[1]
    tok = lax.all_gather(tokens, "gx", axis=0, tiled=True)
    n = tok.shape[0]
    ids = lax.all_gather(seeds, "gx", axis=0, tiled=True)
    pick = (ids.reshape(-1)[:, None] == jnp.arange(nbank, dtype=jnp.int32)).astype(BF16)
    rows = jnp.concatenate([tok, bank], axis=0)
    pre = jnp.concatenate([dot(rows, gate_w), dot(rows, up_w)], axis=1)
    made = lax.psum(pre[n:], "gy").astype(BF16)
    pre = lax.psum_scatter(pre[:n], "gy", scatter_dimension=0, tiled=True).astype(BF16)
    pre = lax.all_gather(pre, "gy", axis=0, tiled=True)
    g = pre[:, :ff].astype(F32)
    u = pre[:, ff:].astype(F32)
    made = dot(pick, made).reshape(n, probes, 2 * ff)
    pg, pu = made[..., :ff], made[..., ff:]
    s = jax.nn.sigmoid(g)
    act = g * s
    slope = s * (1.0 + g * (1.0 - s))
    bend = s * (1.0 - s) * (2.0 + g * (1.0 - 2.0 * s))
    su = slope * u
    hidden = jnp.concatenate(
        [(act * u)[:, None], su[:, None] * pg + act[:, None] * pu], axis=1
    ).astype(BF16)
    outputs = lax.psum_scatter(
        dot(hidden.reshape(-1, ff), down_w).reshape(n, probes + 1, width),
        "gx", scatter_dimension=0, tiled=True,
    )
    student_out = outputs[:, 0].astype(BF16)
    cot = ((outputs[:, 1:] - teacher.astype(F32)) / math.sqrt(probes * n)).astype(BF16)
    cot = lax.all_gather(cot, "gx", axis=0, tiled=True).reshape(-1, width)
    grad_down = contract_rows(hidden[:, 1:].reshape(-1, ff), cot).astype(BF16)
    hc = lax.dot_general(cot, down_w, (((1,), (1,)), ((), ())), preferred_element_type=F32)
    hc = hc.reshape(n, probes, ff)
    a = jnp.sum(hc * pg, axis=1)
    b = jnp.sum(hc * pu, axis=1)
    seg_g = contract_rows(pick, (hc * su[:, None]).astype(BF16).reshape(-1, ff))
    seg_u = contract_rows(pick, (hc * act[:, None]).astype(BF16).reshape(-1, ff))
    seg = lax.psum(jnp.concatenate([seg_g, seg_u], axis=1), "gy").astype(BF16)
    back = lax.psum_scatter(
        jnp.concatenate([a, b], axis=1), "gy", scatter_dimension=0, tiled=True
    ).astype(BF16)
    back = lax.all_gather(back, "gy", axis=0, tiled=True)
    a, b = back[:, :ff].astype(F32), back[:, ff:].astype(F32)
    gate_cot = jnp.concatenate([(bend * u * a + slope * b).astype(BF16), seg[:, :ff]], axis=0)
    up_cot = jnp.concatenate([(slope * a).astype(BF16), seg[:, ff:]], axis=0)
    grad_gate = contract_rows(rows, gate_cot).astype(BF16)
    grad_up = contract_rows(rows, up_cot).astype(BF16)
    return student_out, grad_gate, grad_up, grad_down


def solution(mesh):
    in_specs = (
        P("gx", "gy"),
        P("gx", None),
        P(None, "gy"),
        P("gx", None, "gy"),
        P("gy", "gx"),
        P("gy", "gx"),
        P("gx", "gy"),
    )
    out_specs = (P("gx", "gy"), P("gy", "gx"), P("gy", "gx"), P("gx", "gy"))
    return jax.shard_map(
        on_device, mesh=mesh, in_specs=in_specs, out_specs=out_specs, check_vma=False
    )
```

```python
import functools
import math

import jax
import jax.numpy as jnp
from jax import lax
from jax.experimental import pallas as pl
from jax.experimental.pallas import tpu as pltpu
from jax.sharding import PartitionSpec as P

F32 = jnp.float32
BF16 = jnp.bfloat16
MESH = pl.DeviceIdType.MESH
LANE = 128

TOK, PICK, BANK_SUM, PRE_SUM, BANK_ALL, PRE_ALL, OUT_SUM, COT, BACK_SUM, SEG_SUM, BACK_ALL, SEG_ALL = range(12)


def dot(a, b):
    return jnp.dot(a, b, preferred_element_type=F32)


def dot_t(a, b):
    return lax.dot_general(a, b, (((1,), (1,)), ((), ())), preferred_element_type=F32)


def t_dot(a, b):
    return lax.dot_general(a, b, (((0,), (0,)), ((), ())), preferred_element_type=F32)


def lanes(tile):
    return pl.ds(pl.multiple_of(tile * LANE, LANE), LANE)


def each(count, body):
    def step(i, carry):
        body(i)
        return carry

    lax.fori_loop(0, count, step, 0)


def kernel(
    n, probes, scale,
    tok_ref, pick_ref, bank_ref, teach_ref, gw_ref, uw_ref, dw_ref,
    so_ref, gg_ref, gu_ref, gd_ref,
    tok_all, pick_all, bank_part, bank_recv, pre_send, pre_recv, pre_all, pgu, su_s, act_s,
    hidden, out_send, out_recv, cot_all, hc_s, back_send, back_recv, seg_acc, seg_send, seg_recv,
    gc_all, xt, send_sem, recv_sem,
):
    mx, my = lax.axis_index("gx"), lax.axis_index("gy")
    t, width = tok_ref.shape
    nbank = bank_ref.shape[0]
    ff = gw_ref.shape[1]
    nf = ff // LANE
    tiles = 2 * nf
    rows = n * t
    kt = probes * t
    group = n // 4

    def others(me, body):
        def step(d, carry):
            body(lax.rem(me + d, n))
            return carry

        lax.fori_loop(1, n, step, 0)

    def send(which, axis, me, to, src, dst):
        pltpu.make_async_remote_copy(
            src_ref=src, dst_ref=dst, send_sem=send_sem.at[which, to], recv_sem=recv_sem.at[which, me],
            device_id={axis: to}, device_id_type=MESH,
        ).start()

    def arrived(which, axis, source, ref):
        pltpu.make_async_remote_copy(
            src_ref=ref, dst_ref=ref, send_sem=send_sem.at[which, source],
            recv_sem=recv_sem.at[which, source], device_id={axis: source}, device_id_type=MESH,
        ).wait_recv()

    def sent(which, axis, to, ref):
        pltpu.make_async_remote_copy(
            src_ref=ref, dst_ref=ref, send_sem=send_sem.at[which, to],
            recv_sem=recv_sem.at[which, to], device_id={axis: to}, device_id_type=MESH,
        ).wait_send()

    def part(ref, q):
        return ref.at[pl.ds(pl.multiple_of(q * t, t), t)]

    def bank_tile(ref, j):
        return ref.at[pl.ds(rows, nbank), lanes(j)]

    barrier = pltpu.get_barrier_semaphore()

    def greet(p):
        pl.semaphore_signal(barrier, inc=1, device_id={"gx": p}, device_id_type=MESH)

    def greet_y(p):
        pl.semaphore_signal(barrier, inc=1, device_id={"gy": p}, device_id_type=MESH)

    others(mx, greet)
    others(my, greet_y)

    bank_part_rows = bank_ref[...]

    def bank_step(f):
        bank_part[f] = dot(bank_part_rows, gw_ref[:, lanes(f)]).astype(BF16)
        bank_part[nf + f] = dot(bank_part_rows, uw_ref[:, lanes(f)]).astype(BF16)

    each(nf, bank_step)
    tail = pl.ds(rows + nbank, LANE - nbank)
    pre_all[tail] = jnp.zeros((LANE - nbank, 2 * ff), BF16)
    gc_all[tail] = jnp.zeros((LANE - nbank, 2 * ff), BF16)
    seg_acc[...] = jnp.zeros_like(seg_acc)
    tok_all[mx] = tok_ref[...]
    pick_all[mx] = pick_ref[...]

    pl.semaphore_wait(barrier, 2 * (n - 1))

    others(mx, lambda p: send(TOK, "gx", mx, p, tok_ref, tok_all.at[mx]))

    def send_bank(p):
        @pl.when(p < tiles)
        def _():
            send(BANK_SUM, "gy", my, p, bank_part.at[p], bank_recv.at[my])

    others(my, send_bank)
    others(mx, lambda p: send(PICK, "gx", mx, p, pick_ref, pick_all.at[mx]))

    @pl.when(my < tiles)
    def _():
        bank_recv[my] = bank_part[my]

    others(mx, lambda p: arrived(TOK, "gx", p, tok_all.at[p]))
    half = n // 2

    def pre_step(h):
        first = lax.rem(my // half + h, 2) * half
        x = tok_all[pl.ds(first, half)].reshape(half * t, width)
        at = pl.ds(pl.multiple_of(first * t, half * t), half * t)
        pre_send[at, pl.ds(0, ff)] = dot(x, gw_ref[...]).astype(BF16)
        pre_send[at, pl.ds(ff, ff)] = dot(x, uw_ref[...]).astype(BF16)

        def go(g):
            q = first + g

            @pl.when(q != my)
            def _():
                send(PRE_SUM, "gy", my, q, part(pre_send, q), pre_recv.at[my])

        each(half, go)

    each(2, pre_step)
    pre_recv[my] = part(pre_send, my)[...]

    @pl.when(my < tiles)
    def _():
        others(my, lambda p: arrived(BANK_SUM, "gy", p, bank_recv.at[p]))
        total = bank_recv[0].astype(F32)
        for q in range(1, n):
            total += bank_recv[q].astype(F32)
        bank_tile(pre_all, my)[...] = total.astype(BF16)
        others(my, lambda p: send(BANK_ALL, "gy", my, p, bank_tile(pre_all, my), bank_tile(pre_all, my)))

    x = jnp.concatenate(
        [
            tok_all[...].reshape(rows, width),
            bank_ref[...],
            jnp.zeros((LANE - nbank, width), BF16),
        ],
        axis=0,
    )
    xt[...] = x.T

    others(my, lambda p: arrived(PRE_SUM, "gy", p, pre_recv.at[p]))
    total = pre_recv[0].astype(F32)
    for q in range(1, n):
        total += pre_recv[q].astype(F32)
    part(pre_all, my)[...] = total.astype(BF16)
    others(my, lambda p: send(PRE_ALL, "gy", my, p, part(pre_all, my), part(pre_all, my)))

    def bank_wait(p):
        @pl.when(p < tiles)
        def _():
            arrived(BANK_ALL, "gy", p, bank_tile(pre_all, p))

    others(my, bank_wait)
    block = group * t

    def block_wait(which, axis, me, b, view):
        for g in range(group):
            q = b * group + g

            @pl.when(q != me)
            def _():
                arrived(which, axis, q, view(q))

    def hidden_block(s):
        b = lax.rem(mx // group + s, 4)
        first = b * group
        block_wait(PRE_ALL, "gy", my, b, lambda q: part(pre_all, q))
        block_wait(PICK, "gx", mx, b, lambda q: pick_all.at[q])
        at = pl.ds(pl.multiple_of(b * block, block), block)
        picks = pick_all[pl.ds(first, group)].reshape(group * kt, LANE)
        made = pl.ds(pl.multiple_of(b * group * kt, group * kt), group * kt)
        bank_rows = pl.ds(rows, LANE)

        def tile(f):
            g = pre_all[at, lanes(f)].astype(F32)
            u = pre_all[at, lanes(nf + f)].astype(F32)
            pg = dot(picks, pre_all[bank_rows, lanes(f)])
            pu = dot(picks, pre_all[bank_rows, lanes(nf + f)])
            pgu[made, lanes(f)] = pg.astype(BF16)
            pgu[made, lanes(nf + f)] = pu.astype(BF16)
            sig = jax.nn.sigmoid(g)
            act = g * sig
            su = sig * (1.0 + g * (1.0 - sig)) * u
            su_s[at, lanes(f)] = su
            act_s[at, lanes(f)] = act
            hidden[pl.ds(first, group), 0, :, lanes(f)] = (act * u).astype(BF16).reshape(group, t, LANE)
            shape = (group, probes, t, LANE)
            rest = su.reshape(group, 1, t, LANE) * pg.reshape(shape) + act.reshape(
                group, 1, t, LANE
            ) * pu.reshape(shape)
            hidden[pl.ds(first, group), pl.ds(1, probes), :, lanes(f)] = rest.astype(BF16)

        each(nf, tile)
        h = hidden[pl.ds(first, group)].reshape(group * (probes + 1) * t, ff)
        out_send[pl.ds(first, group)] = (
            dot(h, dw_ref[...]).astype(BF16).reshape(group, probes + 1, t, width)
        )
        for g in range(group):
            q = first + g

            @pl.when(q != mx)
            def _():
                send(OUT_SUM, "gx", mx, q, out_send.at[q], out_recv.at[mx])

    each(4, hidden_block)

    out_recv[mx] = out_send[mx]
    others(mx, lambda p: arrived(OUT_SUM, "gx", p, out_recv.at[p]))
    for k in range(probes + 1):
        total = out_recv[0, k].astype(F32)
        for q in range(1, n):
            total += out_recv[q, k].astype(F32)
        if k == 0:
            so_ref[...] = total.astype(BF16)
        else:
            cot_all[mx, pl.ds((k - 1) * t, t)] = (
                (total - teach_ref[k - 1].astype(F32)) / scale
            ).astype(BF16)
    others(mx, lambda p: send(COT, "gx", mx, p, cot_all.at[mx], cot_all.at[mx]))

    def back_block(s):
        b = lax.rem(my // group + s, 4)
        first = b * group
        block_wait(COT, "gx", mx, b, lambda q: cot_all.at[q])
        at = pl.ds(pl.multiple_of(b * block, block), block)
        made = pl.ds(pl.multiple_of(b * group * kt, group * kt), group * kt)
        hc_s[...] = dot_t(cot_all[pl.ds(first, group)].reshape(group * kt, width), dw_ref[...])
        picks_t = pick_all[pl.ds(first, group)].reshape(group * kt, LANE).T

        def tile(f):
            shape = (group, probes, t, LANE)
            hc = hc_s[:, lanes(f)].reshape(shape)
            pg = pgu[made, lanes(f)].astype(F32).reshape(shape)
            pu = pgu[made, lanes(nf + f)].astype(F32).reshape(shape)
            back_send[at, lanes(f)] = jnp.sum(hc * pg, axis=1).reshape(block, LANE).astype(BF16)
            back_send[at, lanes(nf + f)] = jnp.sum(hc * pu, axis=1).reshape(block, LANE).astype(BF16)
            su = su_s[at, lanes(f)].reshape(group, 1, t, LANE)
            act = act_s[at, lanes(f)].reshape(group, 1, t, LANE)
            seg_acc[:, lanes(f)] += dot(picks_t, (hc * su).reshape(group * kt, LANE).astype(BF16))
            seg_acc[:, lanes(nf + f)] += dot(picks_t, (hc * act).reshape(group * kt, LANE).astype(BF16))

        each(nf, tile)
        for g in range(group):
            q = first + g

            @pl.when(q != my)
            def _():
                send(BACK_SUM, "gy", my, q, part(back_send, q), back_recv.at[my])

    each(4, back_block)
    for j in range(tiles):
        seg_send[j] = seg_acc[pl.ds(0, nbank), pl.ds(j * LANE, LANE)].astype(BF16)

    def send_seg(p):
        @pl.when(p < tiles)
        def _():
            send(SEG_SUM, "gy", my, p, seg_send.at[p], seg_recv.at[my])

    others(my, send_seg)

    @pl.when(my < tiles)
    def _():
        seg_recv[my] = seg_send[my]

    back_recv[my] = part(back_send, my)[...]

    def down_step(f):
        h = hidden[:, pl.ds(1, probes), :, lanes(f)].reshape(n * kt, LANE)
        gd_ref[lanes(f), :] = t_dot(h, cot_all[...].reshape(n * kt, width)).astype(BF16)

    each(nf, down_step)

    others(my, lambda p: arrived(BACK_SUM, "gy", p, back_recv.at[p]))
    total = back_recv[0].astype(F32)
    for q in range(1, n):
        total += back_recv[q].astype(F32)
    a, bb = total[:, :ff], total[:, ff:]
    own = part(pre_all, my)
    g = own[:, pl.ds(0, ff)].astype(F32)
    u = own[:, pl.ds(ff, ff)].astype(F32)
    sig = jax.nn.sigmoid(g)
    slope = sig * (1.0 + g * (1.0 - sig))
    bend = sig * (1.0 - sig) * (2.0 + g * (1.0 - 2.0 * sig))
    mine = part(gc_all, my)
    mine[:, pl.ds(0, ff)] = (bend * u * a + slope * bb).astype(BF16)
    mine[:, pl.ds(ff, ff)] = (slope * a).astype(BF16)
    others(my, lambda p: send(BACK_ALL, "gy", my, p, part(gc_all, my), part(gc_all, my)))

    @pl.when(my < tiles)
    def _():
        others(my, lambda p: arrived(SEG_SUM, "gy", p, seg_recv.at[p]))
        total = seg_recv[0].astype(F32)
        for q in range(1, n):
            total += seg_recv[q].astype(F32)
        bank_tile(gc_all, my)[...] = total.astype(BF16)
        others(my, lambda p: send(SEG_ALL, "gy", my, p, bank_tile(gc_all, my), bank_tile(gc_all, my)))

    others(my, lambda p: arrived(BACK_ALL, "gy", p, part(gc_all, p)))

    def seg_wait(p):
        @pl.when(p < tiles)
        def _():
            arrived(SEG_ALL, "gy", p, bank_tile(gc_all, p))

    others(my, seg_wait)

    def grad_step(f):
        gg_ref[:, lanes(f)] = dot(xt[...], gc_all[:, lanes(f)]).astype(BF16)
        gu_ref[:, lanes(f)] = dot(xt[...], gc_all[:, lanes(nf + f)]).astype(BF16)

    each(nf, grad_step)

    def drain_x(p):
        sent(TOK, "gx", p, tok_ref)
        sent(PICK, "gx", p, pick_ref)
        sent(OUT_SUM, "gx", p, out_send.at[p])
        sent(COT, "gx", p, cot_all.at[mx])

    def drain_y(p):
        sent(PRE_SUM, "gy", p, part(pre_send, p))
        sent(PRE_ALL, "gy", p, part(pre_all, my))
        sent(BACK_SUM, "gy", p, part(back_send, p))
        sent(BACK_ALL, "gy", p, part(gc_all, my))

        @pl.when(p < tiles)
        def _():
            sent(BANK_SUM, "gy", p, bank_part.at[p])
            sent(SEG_SUM, "gy", p, seg_send.at[p])

        @pl.when(my < tiles)
        def _():
            sent(BANK_ALL, "gy", p, bank_tile(pre_all, my))
            sent(SEG_ALL, "gy", p, bank_tile(gc_all, my))

    others(mx, drain_x)
    others(my, drain_y)


def on_device(tokens, seeds, bank, teacher, gate_w, up_w, down_w):
    n = lax.axis_size("gx")
    t, width = tokens.shape
    probes = seeds.shape[1]
    nbank = bank.shape[0]
    ff = gate_w.shape[1]
    tiles = 2 * ff // LANE
    kt = probes * t
    rows = n * t
    pick = (seeds.T.reshape(kt, 1) == jnp.arange(LANE, dtype=jnp.int32)).astype(BF16)
    teach = jnp.transpose(teacher, (1, 0, 2))
    vmem = pl.BlockSpec(memory_space=pltpu.VMEM)
    return pl.pallas_call(
        functools.partial(kernel, n, probes, math.sqrt(probes * rows)),
        out_shape=(
            jax.ShapeDtypeStruct((t, width), BF16),
            jax.ShapeDtypeStruct((width, ff), BF16),
            jax.ShapeDtypeStruct((width, ff), BF16),
            jax.ShapeDtypeStruct((ff, width), BF16),
        ),
        in_specs=[vmem] * 7,
        out_specs=(vmem,) * 4,
        scratch_shapes=[
            pltpu.VMEM((n, t, width), BF16),
            pltpu.VMEM((n, kt, LANE), BF16),
            pltpu.VMEM((tiles, nbank, LANE), BF16),
            pltpu.VMEM((n, nbank, LANE), BF16),
            pltpu.VMEM((rows, 2 * ff), BF16),
            pltpu.VMEM((n, t, 2 * ff), BF16),
            pltpu.VMEM((rows + LANE, 2 * ff), BF16),
            pltpu.VMEM((n * kt, 2 * ff), BF16),
            pltpu.VMEM((rows, ff), F32),
            pltpu.VMEM((rows, ff), F32),
            pltpu.VMEM((n, probes + 1, t, ff), BF16),
            pltpu.VMEM((n, probes + 1, t, width), BF16),
            pltpu.VMEM((n, probes + 1, t, width), BF16),
            pltpu.VMEM((n, kt, width), BF16),
            pltpu.VMEM((n // 4 * kt, ff), F32),
            pltpu.VMEM((rows, 2 * ff), BF16),
            pltpu.VMEM((n, t, 2 * ff), BF16),
            pltpu.VMEM((LANE, 2 * ff), F32),
            pltpu.VMEM((tiles, nbank, LANE), BF16),
            pltpu.VMEM((n, nbank, LANE), BF16),
            pltpu.VMEM((rows + LANE, 2 * ff), BF16),
            pltpu.VMEM((width, rows + LANE), BF16),
            pltpu.SemaphoreType.DMA((12, n)),
            pltpu.SemaphoreType.DMA((12, n)),
        ],
        compiler_params=pltpu.CompilerParams(
            collective_id=0, has_side_effects=True, vmem_limit_bytes=50 * 1024 * 1024
        ),
        cost_estimate=pl.CostEstimate(flops=5 * 10**9, bytes_accessed=6 * 10**6, transcendentals=0),
    )(tokens, pick, bank, teach, gate_w, up_w, down_w)


def solution(mesh):
    in_specs = (
        P("gx", "gy"),
        P("gx", None),
        P(None, "gy"),
        P("gx", None, "gy"),
        P("gy", "gx"),
        P("gy", "gx"),
        P("gx", "gy"),
    )
    out_specs = (P("gx", "gy"), P("gy", "gx"), P("gy", "gx"), P("gx", "gy"))
    return jax.shard_map(
        on_device, mesh=mesh, in_specs=in_specs, out_specs=out_specs, check_vma=False
    )
```
